256 devices in a mesh: sec: 16 (over z, core), env: 16 (over y, x).
Axes of the slice: x: 4, y: 4, z: 8, core: 2. Of those that a mesh axis runs over, the one named last changes fastest.
Arguments:
- env_left: bfloat16 [32, 40, 128, 128], P('sec', None, 'env'), may hold values from -6 to 6
- env_right: bfloat16 [32, 40, 128, 128], P('sec', None, 'env'), may hold values from -6 to 6
- site_left: bfloat16 [2048, 128, 128], P('sec'), may hold values from -0.25 to 0.25
- site_right: bfloat16 [2048, 128, 128], P('sec'), may hold values from -0.25 to 0.25
- source_left: int32 [2048], P('sec'), may hold values from 0 to 31, as said below
- source_right: int32 [2048], P('sec'), may hold values from 0 to 31, as said below
- channel_left: int32 [2048], P('sec'), may hold values from 0 to 7
- channel_right: int32 [2048], P('sec'), may hold values from 0 to 7
- fanin_left: int32 [32], P('sec'), may hold values from 8 to 64, as said below
- fanin_right: int32 [32], P('sec'), may hold values from 8 to 64, as said below
- operator_table: bfloat16 [8, 40, 40], replicated, may hold values from -1.25 to 1.25
- operator_pattern: int32 [8, 40, 40], replicated, may hold values 0 or 1
Outputs:
- new_left: bfloat16 [32, 40, 128, 128], P('sec', None, 'env')
- new_right: bfloat16 [32, 40, 128, 128], P('sec', None, 'env')
The draws below stay inside these ranges and needn't reach their ends.
Inputs may be any that keep to these rules, and one draw needn't show every extreme that they name: `source_left`: among the 128 slots held by one index of sec, all sources owned by one index q of sec (sectors 2 * q to 2 * q + 1) are one and the same sector. `source_right`: among the 128 slots held by one index of sec, all sources owned by one index q of sec are one and the same sector. `fanin_left`: some sector has all 64 slots live. `fanin_right`: some sector has all 64 slots live.
All inputs are finite; a program needn't handle non-finite values.
Results may differ from the reference program's by a relative error of at most 0.015.
Values may be sent and summed in bfloat16 or wider, within the bound.
A program may use at most 128 MiB of HBM per device.

```python
import jax
import jax.numpy as jnp
from jax import lax

M = 128
W = 40
P_SIZE = 8
SEC_DEV = 2
BLK_SEC = 64
NS = 32
NB = 2048
N_ENV = 16


def sources_for(key, salt):
    owner_count = NS // SEC_DEV
    slot_count = SEC_DEV * BLK_SEC
    base_key = jax.random.fold_in(key, salt)
    key_local, key_used, key_pick = jax.random.split(base_key, 3)
    local_choice = jax.random.randint(key_local, (owner_count, owner_count), 0, SEC_DEV)
    in_use = jax.random.randint(key_used, (owner_count, owner_count), 0, 4) > 0
    in_use = in_use | (jnp.arange(owner_count)[:, None] == jnp.arange(owner_count)[None, :])
    used_count = jnp.sum(in_use.astype(jnp.int32), axis=1)
    picked = jax.random.randint(key_pick, (owner_count, slot_count), 0, used_count[:, None])
    rank_order = jnp.cumsum(in_use.astype(jnp.int32), axis=1) - 1
    matches = in_use[:, None, :] & (rank_order[:, None, :] == picked[:, :, None])
    owners = jnp.sum(matches.astype(jnp.int32) * jnp.arange(owner_count, dtype=jnp.int32)[None, None, :], axis=2)
    local_ids = jnp.take_along_axis(local_choice, owners, axis=1)
    return (owners * SEC_DEV + local_ids).reshape(owner_count * slot_count).astype(jnp.int32)


def fanins_for(key, salt):
    base_key = jax.random.fold_in(key, salt)
    key_level, key_count, key_full = jax.random.split(base_key, 3)
    lowest = BLK_SEC // 8
    levels = jax.random.randint(key_level, (NS,), 0, 3)
    bottom = lowest * jnp.left_shift(jnp.ones((NS,), jnp.int32), levels)
    counts = jax.random.randint(key_count, (NS,), bottom, 2 * bottom + 1)
    full_index = jax.random.randint(key_full, (), 0, NS)
    return jnp.where(jnp.arange(NS) == full_index, BLK_SEC, counts).astype(jnp.int32)


def draw_source_left(key, part):
    return sources_for(key, 11)


def draw_source_right(key, part):
    return sources_for(key, 12)


def draw_fanin_left(key, part):
    return fanins_for(key, 13)


def draw_fanin_right(key, part):
    return fanins_for(key, 14)


def touch_ends(array, key, least, high):
    longest = array.shape.index(max(array.shape))
    spots = []
    for shift in (0, 1):
        where = [jax.random.randint(jax.random.fold_in(key, axis), (), 0, length) for axis, length in enumerate(array.shape)]
        where[longest] = (where[longest] + shift) % array.shape[longest]
        spots.append(tuple(where))
    return array.at[spots[0]].set(least).at[spots[1]].set(high)


def block_scale(own_key, dims, cuts, smallest, top_value):
    factor_of, own = 1.0, jax.random.fold_in(own_key, 6)
    for axis_at, blocks in cuts:
        draws = jnp.exp(jax.random.uniform(jax.random.fold_in(own, axis_at), (blocks,), jnp.float32, smallest / len(cuts), top_value / len(cuts)))
        factor_of = factor_of * jnp.repeat(draws, dims[axis_at] // blocks).reshape([-1 if axis == axis_at else 1 for axis in range(len(dims))])
    return factor_of


def noise(stream_key, extent, spread, bound, shards=(), held_as=jnp.bfloat16):
    result = jax.random.normal(stream_key, extent, jnp.float32) * spread
    if len(shards) > 0:
        result = block_scale(stream_key, extent, shards, -0.22, 0.18) * result
    return jnp.clip(result, min=-bound, max=bound).astype(held_as)


def setup_inputs(seed: int = 0) -> dict:
    arg_keys = jax.random.split(jax.random.key(seed), 13)
    return {
        "env_left": noise(arg_keys[0], (NS, W, M, M), 1.0, 6.0, ((0, 16), (2, 16))),
        "env_right": noise(arg_keys[1], (NS, W, M, M), 1.0, 6.0, ((0, 16), (2, 16))),
        "site_left": noise(arg_keys[2], (NB, M, M), (4 * M) ** -0.5, 0.25, ((0, 16),)),
        "site_right": noise(arg_keys[3], (NB, M, M), (4 * M) ** -0.5, 0.25, ((0, 16),)),
        "source_left": draw_source_left(jax.random.fold_in(arg_keys[12], 71), 0),
        "source_right": draw_source_right(jax.random.fold_in(arg_keys[12], 71), 0),
        "channel_left": touch_ends(jax.random.randint(arg_keys[6], (NB,), 0, P_SIZE), jax.random.fold_in(arg_keys[6], 1), 0, P_SIZE - 1).astype(jnp.int32),
        "channel_right": touch_ends(jax.random.randint(arg_keys[7], (NB,), 0, P_SIZE), jax.random.fold_in(arg_keys[7], 1), 0, P_SIZE - 1).astype(jnp.int32),
        "fanin_left": draw_fanin_left(jax.random.fold_in(arg_keys[12], 71), 0),
        "fanin_right": draw_fanin_right(jax.random.fold_in(arg_keys[12], 71), 0),
        "operator_table": noise(arg_keys[10], (P_SIZE, W, W), (W // 2) ** -0.5, 1.25),
        "operator_pattern": touch_ends((jax.random.randint(arg_keys[11], (P_SIZE, W, W), 0, 2) < 1).astype(jnp.int32), jax.random.fold_in(arg_keys[11], 1), 0, 1),
    }


def side_rebuild(old_tiles, site_blocks, source, channel, fan_in, mixing):
    row_count = M // N_ENV

    def one_sector(sector_index):
        first_slot = sector_index * BLK_SEC
        blocks = lax.dynamic_slice_in_dim(site_blocks, first_slot, BLK_SEC, 0)
        sources = lax.dynamic_slice_in_dim(source, first_slot, BLK_SEC, 0)
        channels = lax.dynamic_slice_in_dim(channel, first_slot, BLK_SEC, 0)
        live_count = lax.dynamic_index_in_dim(fan_in, sector_index, 0, keepdims=False)
        live_mask = jnp.arange(BLK_SEC, dtype=jnp.int32) < live_count
        blocks = jnp.where(live_mask[:, None, None], blocks, jnp.zeros_like(blocks))
        fetched = jnp.take(old_tiles, sources, axis=0)
        mix_slots = jnp.take(mixing, channels, axis=0)
        first_section = jnp.einsum("suma,sac->sumc", fetched.astype(jnp.float32), blocks.astype(jnp.float32)).astype(jnp.bfloat16)
        mixed_section = jnp.einsum("suv,sumc->svmc", mix_slots.astype(jnp.float32), first_section.astype(jnp.float32)).astype(jnp.bfloat16)
        split_blocks = blocks.astype(jnp.float32).reshape(BLK_SEC, N_ENV, row_count, M)
        split_mixed = mixed_section.astype(jnp.float32).reshape(BLK_SEC, W, N_ENV, row_count, M)
        partial_value = jnp.einsum("serc,sverd->evcd", split_blocks, split_mixed).astype(jnp.bfloat16)
        return jnp.sum(partial_value.astype(jnp.float32), axis=0).astype(jnp.bfloat16)

    return lax.map(one_sector, jnp.arange(NS, dtype=jnp.int32))


def reference(env_left, env_right, site_left, site_right, source_left, source_right, channel_left, channel_right, fanin_left, fanin_right, operator_table, operator_pattern):
    operator = (operator_table.astype(jnp.float32) * operator_pattern.astype(jnp.float32)).astype(jnp.bfloat16)
    new_left = side_rebuild(env_left, site_left, source_left, channel_left, fanin_left, operator)
    new_right = side_rebuild(env_right, site_right, source_right, channel_right, fanin_right, jnp.transpose(operator, (0, 2, 1)))
    return (new_left, new_right)
```

```python
import functools

import jax
import jax.numpy as jnp
from jax import lax
from jax.experimental import pallas as pl
from jax.experimental.pallas import tpu as pltpu
from jax.sharding import PartitionSpec as P

MESH = pl.DeviceIdType.MESH
BF, F32 = jnp.bfloat16, jnp.float32
NZ, NX, NY = 8, 4, 4
LAST = NZ - 2
W, R, S = 40, 8, 128
WR = W * R
HALF = WR // 2
SLOTS, CHANNELS = 64, 8


def dot(a, b):
    return lax.dot_general(a, b, (((1,), (0,)), ((), ())), preferred_element_type=F32)


def kernel(
    fan_l, fan_r, src_l, src_r, chn_l, chn_r, srcv_l, srcv_r, table, pattern, env_l, env_r, site_l, site_r,
    out_l, out_r,
    got, site, kron, mixenv, mixed, rows_t, send1, recv1, send2, recv2,
    loc_sem, ring_s, ring_r, cross_s, cross_r, s1_s, s1_r, s2_s, s2_r,
):
    fan, src, chn, srcv = (fan_l, fan_r), (src_l, src_r), (chn_l, chn_r), (srcv_l, srcv_r)
    env_in, site_in, out = (env_l, env_r), (site_l, site_r), (out_l, out_r)
    sec, env = lax.axis_index("sec"), lax.axis_index("env")
    z, core = sec // 2, sec % 2
    y, x = env // NX, env % NX
    other = (z * 2 + 1 - core, env)
    up = (lax.rem(z + 1, NZ) * 2 + core, env)
    down = (lax.rem(z + NZ - 1, NZ) * 2 + core, env)
    x_peer = [(sec, y * NX + lax.rem(x + d, NX)) for d in range(1, NX)]
    y_peer = [(sec, lax.rem(y + d, NY) * NX + x) for d in range(1, NY)]

    barrier = pltpu.get_barrier_semaphore()
    partners = [other, up, down] + x_peer + y_peer
    for peer in partners:
        pl.semaphore_signal(barrier, inc=1, device_id=peer, device_id_type=MESH)
    pl.semaphore_wait(barrier, len(partners))

    def remote(a, b, ssem, rsem, peer):
        return pltpu.make_async_remote_copy(
            src_ref=a, dst_ref=b, send_sem=ssem, recv_sem=rsem, device_id=peer, device_id_type=MESH
        )

    def chunk_of(way, n):
        far = n // 2 + 1
        chip = lax.rem(z + NZ - far, NZ) if way == 0 else lax.rem(z + far, NZ)
        h = n % 2 if n < LAST else way
        return chip, h

    def ring(side, way, n):
        peer = up if way == 0 else down
        if n < 2:
            a, chip, h = env_in[side].at[n], z, n
        else:
            back = n - 2 if (n < LAST or way == 0) else n - 1
            chip, h = chunk_of(way, back)
            a = got.at[side, chip * 2 + core, h]
        return remote(a, got.at[side, chip * 2 + core, h], ring_s.at[side, way, n], ring_r.at[side, way, n], peer)

    def ring_in(side, way, n):
        chip, h = chunk_of(way, n)
        spot = got.at[side, chip * 2 + core, h]
        return remote(spot, spot, ring_s.at[side, way, n], ring_r.at[side, way, n], up if way == 0 else down)

    def cross(side, way, n):
        if way == 2:
            a, chip, h, c = env_in[side].at[n], z, n, n
        else:
            chip, h = chunk_of(way, n)
            a, c = got.at[side, chip * 2 + core, h], 2 + 2 * n + way
        return remote(a, got.at[side, chip * 2 + core, h], cross_s.at[side, c], cross_r.at[side, c], other)

    def cross_in(side, way, n):
        chip, h, c = (z, n, n) if way == 2 else (*chunk_of(way, n), 2 + 2 * n + way)
        spot = got.at[side, chip * 2 + 1 - core, h]
        return remote(spot, spot, cross_s.at[side, c], cross_r.at[side, c], other)

    def gather_start(side):
        for n in range(2):
            ring(side, 0, n).start()
            ring(side, 1, n).start()
        for n in range(2):
            cross(side, 2, n).start()

    def gather_step(side, n):
        for way in range(2):
            ring_in(side, way, n).wait_recv()
            for later in range(2, LAST + 1):
                back = later - 2 if (later < LAST or way == 0) else later - 1
                if back == n:
                    ring(side, way, later).start()
            cross(side, way, n).start()

    def cross_wait(side, n):
        for way in range(2):
            cross_in(side, way, n).wait_recv()

    local = [
        pltpu.make_async_copy(env_in[0], got.at[0, sec], loc_sem.at[0]),
        pltpu.make_async_copy(env_in[1], got.at[1, sec], loc_sem.at[1]),
        pltpu.make_async_copy(site_in[0], site.at[0], loc_sem.at[2]),
        pltpu.make_async_copy(site_in[1], site.at[1], loc_sem.at[3]),
    ]
    gather_start(0)
    for c in local:
        c.start()

    spread = (lax.broadcasted_iota(jnp.int32, (WR, W), 0) >> 3 == lax.broadcasted_iota(jnp.int32, (WR, W), 1))
    spread = spread.astype(F32).astype(BF)
    spread_t = (lax.broadcasted_iota(jnp.int32, (W, WR), 1) >> 3 == lax.broadcasted_iota(jnp.int32, (W, WR), 0))
    spread_t = spread_t.astype(F32).astype(BF)
    same_row = (
        lax.broadcasted_iota(jnp.int32, (WR, WR), 0) & 7 == lax.broadcasted_iota(jnp.int32, (WR, WR), 1) & 7
    )

    def build_kron(side):
        def body(p, carry):
            op = (table[p].astype(F32) * pattern[p].astype(F32)).astype(BF)
            dims = (((1,), (1,)), ((), ())) if side == 0 else (((1,), (0,)), ((), ()))
            tall = lax.dot_general(spread, op, dims, preferred_element_type=F32).astype(BF)
            full = jnp.where(same_row, dot(tall, spread_t), 0.0).astype(BF)
            kron[side, p] = full
            return carry

        lax.fori_loop(0, CHANNELS, body, 0)

    def build_rows(side):
        pair_row = pl.multiple_of(env // 2 * 16, 16)
        upper = (env % 2).astype(F32)
        for k in range(2):
            live = fan[side][k]
            for g in range(SLOTS // 16):
                block = site[side, pl.ds(k * SLOTS + g * 16, 16), pl.ds(pair_row, 16), :].astype(F32)
                mine = block[:, :R] * (1.0 - upper) + block[:, R:] * upper
                slot = g * 16 + lax.broadcasted_iota(jnp.int32, (16, R, S), 0)
                mine = jnp.where(slot < live, mine, 0.0)
                rows_t[side, k, :, g * 128 : (g + 1) * 128] = mine.reshape(16 * R, S).T.astype(BF)

    def pick(side, q):
        odd = jnp.max((srcv[side][...] == 2 * q + 1).astype(F32), axis=1, keepdims=True)
        return (got[side, q, 0].astype(F32) * (1.0 - odd) + got[side, q, 1].astype(F32) * odd).astype(BF)

    def mix_chip(side, chip):
        rhs = jnp.concatenate([pick(side, chip * 2), pick(side, chip * 2 + 1)], axis=1)

        def body(p, carry):
            r = dot(kron[side, p], rhs).astype(BF)
            mixenv[chip * 2 * CHANNELS + p] = r[:, :S]
            mixenv[(chip * 2 + 1) * CHANNELS + p] = r[:, S:]
            return carry

        lax.fori_loop(0, CHANNELS, body, 0)

    zero = jnp.zeros((S, S), BF)

    def multiply(side, k, lo, hi):
        def body(pair, carry):
            j = k * SLOTS + 2 * pair
            i0 = (src[side][j] >> 1) * CHANNELS + chn[side][j]
            i1 = (src[side][j + 1] >> 1) * CHANNELS + chn[side][j + 1]
            lhs = jnp.concatenate([mixenv[i0], mixenv[i1]], axis=1)
            rhs = jnp.concatenate(
                [
                    jnp.concatenate([site[side, j], zero], axis=1),
                    jnp.concatenate([zero, site[side, j + 1]], axis=1),
                ],
                axis=0,
            )
            r = dot(lhs, rhs)
            both = jnp.concatenate([r[:, :S].reshape(W, R, S), r[:, S:].reshape(W, R, S)], axis=1)
            mixed[:, pl.ds(pl.multiple_of(pair * 16, 16), 16), :] = both.astype(BF)
            return carry

        lax.fori_loop(lo, hi, body, 0)

    def contract(side, k, half):
        u = side * 2 + k

        def body(i, carry):
            v = half * (W // 2) + 2 * i
            r = dot(rows_t[side, k], jnp.concatenate([mixed[v], mixed[v + 1]], axis=1))
            rows = pl.ds(pl.multiple_of(i * 16, 16), 16)
            for e in range(NX * NY):
                t = r[e * R : (e + 1) * R]
                t = jnp.concatenate([t[:, :S], t[:, S:]], axis=0).astype(BF)
                a, b = (e % NX, e // NX) if half == 0 else (e // NX, e % NX)
                send1[u, half, a, b, rows, :] = t
            return carry

        lax.fori_loop(0, W // 4, body, 0)

    def first_copy(u, half, d):
        mine = x if half == 0 else y
        peer = x_peer[d] if half == 0 else y_peer[d]
        return remote(
            send1.at[u, half, lax.rem(mine + d + 1, 4)], recv1.at[u, half, d],
            s1_s.at[u, half, d], s1_r.at[u, half, d], peer,
        )

    def second_copy(u, half, d):
        mine = y if half == 0 else x
        peer = y_peer[d] if half == 0 else x_peer[d]
        return remote(
            send2.at[u, half, lax.rem(mine + d + 1, 4)], recv2.at[u, half, d],
            s2_s.at[u, half, d], s2_r.at[u, half, d], peer,
        )

    def send_first(u, half):
        for d in range(3):
            first_copy(u, half, d).start()

    def sum_first(u):
        for half in range(2):
            mine = x if half == 0 else y
            for d in range(3):
                first_copy(u, half, d).wait_recv()

            def body(b, carry, half=half, mine=mine):
                t = send1[u, half, mine, b].astype(F32)
                for d in range(3):
                    t = t + recv1[u, half, d, b].astype(F32)
                send2[u, half, b] = t.astype(BF)
                return carry

            lax.fori_loop(0, 4, body, 0)
            for d in range(3):
                second_copy(u, half, d).start()

    def sum_second(u):
        for half in range(2):
            mine = y if half == 0 else x
            t = send2[u, half, mine].astype(F32)
            for d in range(3):
                second_copy(u, half, d).wait_recv()
                t = t + recv2[u, half, d].astype(F32)
            out[u // 2][u % 2, half * HALF : (half + 1) * HALF, :] = t.astype(BF)

    build_kron(0)
    build_kron(1)
    local[0].wait()
    cross_in(0, 2, 0).wait_recv()
    cross_in(0, 2, 1).wait_recv()
    mix_chip(0, z)
    for n in range(LAST + 1):
        gather_step(0, n)
        if n == 0:
            local[2].wait()
            build_rows(0)
        if n == 2:
            local[3].wait()
            build_rows(1)
        if n == LAST - 1:
            gather_start(1)
        if n % 2 == 1:
            cross_wait(0, n - 1)
            cross_wait(0, n)
            mix_chip(0, lax.rem(z + NZ - n // 2 - 1, NZ))
            mix_chip(0, lax.rem(z + n // 2 + 1, NZ))
    cross_wait(0, LAST)
    mix_chip(0, lax.rem(z + NZ // 2, NZ))

    for seg in range(4):
        multiply(0, 0, seg * 8, seg * 8 + 8)
        gather_step(1, seg)
    contract(0, 0, 0)
    send_first(0, 0)
    contract(0, 0, 1)
    send_first(0, 1)
    for seg in range(4):
        multiply(0, 1, seg * 8, seg * 8 + 8)
        if seg < 3:
            gather_step(1, seg + 4)
    contract(0, 1, 0)
    send_first(1, 0)
    contract(0, 1, 1)
    send_first(1, 1)

    local[1].wait()
    for n in range(2):
        cross_in(1, 2, n).wait_recv()
    for n in range(LAST + 1):
        cross_wait(1, n)
    sum_first(0)

    def mix_right(lo, hi):
        def body(chip, carry):
            mix_chip(1, chip)
            return carry

        lax.fori_loop(lo, hi, body, 0)

    mix_right(0, NZ // 2)
    sum_first(1)
    mix_right(NZ // 2, NZ)
    for k in range(2):
        multiply(1, k, 0, 32)
        for half in range(2):
            contract(1, k, half)
            send_first(2 + k, half)
        sum_second(k)
    for u in (2, 3):
        sum_first(u)
    for u in (2, 3):
        sum_second(u)

    for side in range(2):
        for n in range(LAST + 1):
            for way in range(2):
                ring(side, way, n).wait_send()
                cross(side, way, n).wait_send()
        for n in range(2):
            cross(side, 2, n).wait_send()
    for u in range(4):
        for half in range(2):
            for d in range(3):
                first_copy(u, half, d).wait_send()
                second_copy(u, half, d).wait_send()


def per_device(
    env_left, env_right, site_left, site_right, source_left, source_right, channel_left, channel_right,
    fanin_left, fanin_right, operator_table, operator_pattern,
):
    smem = pl.BlockSpec(memory_space=pltpu.SMEM)
    vmem = pl.BlockSpec(memory_space=pltpu.VMEM)
    hbm = pl.BlockSpec(memory_space=pl.ANY)
    dma = pltpu.SemaphoreType.DMA
    new_left, new_right = pl.pallas_call(
        kernel,
        out_shape=[jax.ShapeDtypeStruct((2, WR, S), BF)] * 2,
        in_specs=[smem] * 6 + [vmem] * 4 + [hbm] * 4,
        out_specs=[vmem, vmem],
        scratch_shapes=[
            pltpu.VMEM((2, 2 * NZ, 2, WR, S), BF),
            pltpu.VMEM((2, 2 * SLOTS, S, S), BF),
            pltpu.VMEM((2, CHANNELS, WR, WR), BF),
            pltpu.VMEM((2 * NZ * CHANNELS, WR, S), BF),
            pltpu.VMEM((W, SLOTS * R, S), BF),
            pltpu.VMEM((2, 2, S, SLOTS * R), BF),
            pltpu.VMEM((4, 2, 4, 4, HALF, S), BF),
            pltpu.VMEM((4, 2, 3, 4, HALF, S), BF),
            pltpu.VMEM((4, 2, 4, HALF, S), BF),
            pltpu.VMEM((4, 2, 3, HALF, S), BF),
            dma((4,)),
            dma((2, 2, LAST + 1)),
            dma((2, 2, LAST + 1)),
            dma((2, 2 * NZ)),
            dma((2, 2 * NZ)),
            dma((4, 2, 3)),
            dma((4, 2, 3)),
            dma((4, 2, 3)),
            dma((4, 2, 3)),
        ],
        compiler_params=pltpu.CompilerParams(
            collective_id=0, has_side_effects=True, vmem_limit_bytes=60 * 2**20
        ),
    )(
        fanin_left, fanin_right, source_left, source_right, channel_left, channel_right,
        source_left.reshape(1, -1), source_right.reshape(1, -1), operator_table, operator_pattern,
        env_left.reshape(2, WR, S), env_right.reshape(2, WR, S), site_left, site_right,
    )
    return new_left.reshape(2, W, R, S), new_right.reshape(2, W, R, S)


def solution(mesh):
    wide, flat = P("sec", None, "env", None), P("sec")
    return jax.shard_map(
        per_device,
        mesh=mesh,
        in_specs=(wide, wide, P("sec", None, None), P("sec", None, None)) + (flat,) * 6 + (P(), P()),
        out_specs=(wide, wide),
        check_vma=False,
    )
```

```python
import functools

import jax
import jax.numpy as jnp
from jax import lax
from jax.experimental import pallas as pl
from jax.experimental.pallas import tpu as pltpu
from jax.sharding import PartitionSpec as P

MESH = pl.DeviceIdType.MESH
BF, F32 = jnp.bfloat16, jnp.float32
NZ, NX, NY = 8, 4, 4
LAST = NZ - 2
W, R, S = 40, 8, 128
WR = W * R
HALF = WR // 2
SLOTS, CHANNELS = 64, 8


def dot(a, b):
    return lax.dot_general(a, b, (((1,), (0,)), ((), ())), preferred_element_type=F32)


def kernel(
    fan_l, fan_r, src_l, src_r, chn_l, chn_r, srcv_l, srcv_r, table, pattern, env_l, env_r, site_l, site_r,
    out_l, out_r,
    got, site, kron, mixenv, mixed, rows_t, send1, recv1, send2, recv2,
    loc_sem, ring_s, ring_r, cross_s, cross_r, s1_s, s1_r, s2_s, s2_r,
):
    fan, src, chn, srcv = (fan_l, fan_r), (src_l, src_r), (chn_l, chn_r), (srcv_l, srcv_r)
    env_in, site_in, out = (env_l, env_r), (site_l, site_r), (out_l, out_r)
    sec, env = lax.axis_index("sec"), lax.axis_index("env")
    z, core = sec // 2, sec % 2
    y, x = env // NX, env % NX
    other = (z * 2 + 1 - core, env)
    up = (lax.rem(z + 1, NZ) * 2 + core, env)
    down = (lax.rem(z + NZ - 1, NZ) * 2 + core, env)
    x_peer = [(sec, y * NX + lax.rem(x + d, NX)) for d in range(1, NX)]
    y_peer = [(sec, lax.rem(y + d, NY) * NX + x) for d in range(1, NY)]

    barrier = pltpu.get_barrier_semaphore()
    partners = [other, up, down] + x_peer + y_peer
    for peer in partners:
        pl.semaphore_signal(barrier, inc=1, device_id=peer, device_id_type=MESH)
    pl.semaphore_wait(barrier, len(partners))

    def remote(a, b, ssem, rsem, peer):
        return pltpu.make_async_remote_copy(
            src_ref=a, dst_ref=b, send_sem=ssem, recv_sem=rsem, device_id=peer, device_id_type=MESH
        )

    def chunk_of(way, n):
        far = n // 2 + 1
        chip = lax.rem(z + NZ - far, NZ) if way == 0 else lax.rem(z + far, NZ)
        h = n % 2 if n < LAST else way
        return chip, h

    def ring(side, way, n):
        peer = up if way == 0 else down
        if n < 2:
            a, chip, h = env_in[side].at[n], z, n
        else:
            back = n - 2 if (n < LAST or way == 0) else n - 1
            chip, h = chunk_of(way, back)
            a = got.at[side, chip * 2 + core, h]
        return remote(a, got.at[side, chip * 2 + core, h], ring_s.at[side, way, n], ring_r.at[side, way, n], peer)

    def ring_in(side, way, n):
        chip, h = chunk_of(way, n)
        spot = got.at[side, chip * 2 + core, h]
        return remote(spot, spot, ring_s.at[side, way, n], ring_r.at[side, way, n], up if way == 0 else down)

    def cross(side, way, n):
        if way == 2:
            a, chip, h, c = env_in[side].at[n], z, n, n
        else:
            chip, h = chunk_of(way, n)
            a, c = got.at[side, chip * 2 + core, h], 2 + 2 * n + way
        return remote(a, got.at[side, chip * 2 + core, h], cross_s.at[side, c], cross_r.at[side, c], other)

    def cross_in(side, way, n):
        chip, h, c = (z, n, n) if way == 2 else (*chunk_of(way, n), 2 + 2 * n + way)
        spot = got.at[side, chip * 2 + 1 - core, h]
        return remote(spot, spot, cross_s.at[side, c], cross_r.at[side, c], other)

    def gather_start(side):
        for n in range(2):
            ring(side, 0, n).start()
            ring(side, 1, n).start()
        for n in range(2):
            cross(side, 2, n).start()

    def gather_step(side, n):
        for way in range(2):
            ring_in(side, way, n).wait_recv()
            for later in range(2, LAST + 1):
                back = later - 2 if (later < LAST or way == 0) else later - 1
                if back == n:
                    ring(side, way, later).start()
            cross(side, way, n).start()

    def cross_wait(side, n):
        for way in range(2):
            cross_in(side, way, n).wait_recv()

    local = [
        pltpu.make_async_copy(env_in[0], got.at[0, sec], loc_sem.at[0]),
        pltpu.make_async_copy(env_in[1], got.at[1, sec], loc_sem.at[1]),
        pltpu.make_async_copy(site_in[0], site.at[0], loc_sem.at[2]),
        pltpu.make_async_copy(site_in[1], site.at[1], loc_sem.at[3]),
    ]
    gather_start(0)
    for c in local:
        c.start()

    spread = (lax.broadcasted_iota(jnp.int32, (WR, W), 0) >> 3 == lax.broadcasted_iota(jnp.int32, (WR, W), 1))
    spread = spread.astype(F32).astype(BF)
    spread_t = (lax.broadcasted_iota(jnp.int32, (W, WR), 1) >> 3 == lax.broadcasted_iota(jnp.int32, (W, WR), 0))
    spread_t = spread_t.astype(F32).astype(BF)
    same_row = (
        lax.broadcasted_iota(jnp.int32, (WR, WR), 0) & 7 == lax.broadcasted_iota(jnp.int32, (WR, WR), 1) & 7
    )

    def build_kron(side):
        def body(p, carry):
            op = (table[p].astype(F32) * pattern[p].astype(F32)).astype(BF)
            dims = (((1,), (1,)), ((), ())) if side == 0 else (((1,), (0,)), ((), ()))
            tall = lax.dot_general(spread, op, dims, preferred_element_type=F32).astype(BF)
            full = jnp.where(same_row, dot(tall, spread_t), 0.0).astype(BF)
            kron[side, p] = full
            return carry

        lax.fori_loop(0, CHANNELS, body, 0)

    def build_rows(side):
        pair_row = pl.multiple_of(env // 2 * 16, 16)
        upper = (env % 2).astype(F32)
        for k in range(2):
            live = fan[side][k]
            for g in range(SLOTS // 16):
                block = site[side, pl.ds(k * SLOTS + g * 16, 16), pl.ds(pair_row, 16), :].astype(F32)
                mine = block[:, :R] * (1.0 - upper) + block[:, R:] * upper
                slot = g * 16 + lax.broadcasted_iota(jnp.int32, (16, R, S), 0)
                mine = jnp.where(slot < live, mine, 0.0)
                rows_t[side, k, :, g * 128 : (g + 1) * 128] = mine.reshape(16 * R, S).T.astype(BF)

    def pick(side, q):
        odd = jnp.max((srcv[side][...] == 2 * q + 1).astype(F32), axis=1, keepdims=True)
        return (got[side, q, 0].astype(F32) * (1.0 - odd) + got[side, q, 1].astype(F32) * odd).astype(BF)

    def mix_chip(side, chip):
        rhs = jnp.concatenate([pick(side, chip * 2), pick(side, chip * 2 + 1)], axis=1)

        def body(p, carry):
            r = dot(kron[side, p], rhs).astype(BF)
            mixenv[chip * 2 * CHANNELS + p] = r[:, :S]
            mixenv[(chip * 2 + 1) * CHANNELS + p] = r[:, S:]
            return carry

        lax.fori_loop(0, CHANNELS, body, 0, unroll=True)

    def multiply(side, k, hooks=()):
        def part(seg, carry):
            for i in range(8):
                pair = seg * 8 + i
                j = k * SLOTS + 2 * pair
                i0 = (src[side][j] >> 1) * CHANNELS + chn[side][j]
                i1 = (src[side][j + 1] >> 1) * CHANNELS + chn[side][j + 1]
                r0 = dot(mixenv[i0], site[side, j]).reshape(W, R, S)
                r1 = dot(mixenv[i1], site[side, j + 1]).reshape(W, R, S)
                both = jnp.concatenate([r0, r1], axis=1).astype(BF)
                mixed[:, pl.ds(pl.multiple_of(pair * 16, 16), 16), :] = both
            for i, hook in enumerate(hooks):
                pl.when(seg == i)(hook)
            return carry

        lax.fori_loop(0, SLOTS // 16, part, 0)

    def contract(side, k, half):
        u = side * 2 + k

        def body(i, carry):
            v = half * (W // 2) + 2 * i
            r = dot(rows_t[side, k], jnp.concatenate([mixed[v], mixed[v + 1]], axis=1))
            rows = pl.ds(pl.multiple_of(i * 16, 16), 16)
            for e in range(NX * NY):
                t = r[e * R : (e + 1) * R]
                t = jnp.concatenate([t[:, :S], t[:, S:]], axis=0).astype(BF)
                a, b = (e % NX, e // NX) if half == 0 else (e // NX, e % NX)
                send1[u, half, a, b, rows, :] = t
            return carry

        lax.fori_loop(0, W // 4, body, 0, unroll=True)

    def first_copy(u, half, d):
        mine = x if half == 0 else y
        peer = x_peer[d] if half == 0 else y_peer[d]
        return remote(
            send1.at[u, half, lax.rem(mine + d + 1, 4)], recv1.at[u, half, d],
            s1_s.at[u, half, d], s1_r.at[u, half, d], peer,
        )

    def second_copy(u, half, d):
        mine = y if half == 0 else x
        peer = y_peer[d] if half == 0 else x_peer[d]
        return remote(
            send2.at[u, half, lax.rem(mine + d + 1, 4)], recv2.at[u, half, d],
            s2_s.at[u, half, d], s2_r.at[u, half, d], peer,
        )

    def send_first(u, half):
        for d in range(3):
            first_copy(u, half, d).start()

    def sum_first(u):
        for half in range(2):
            mine = x if half == 0 else y
            for d in range(3):
                first_copy(u, half, d).wait_recv()

            def body(b, carry, half=half, mine=mine):
                t = send1[u, half, mine, b].astype(F32)
                for d in range(3):
                    t = t + recv1[u, half, d, b].astype(F32)
                send2[u, half, b] = t.astype(BF)
                return carry

            lax.fori_loop(0, 4, body, 0)
            for d in range(3):
                second_copy(u, half, d).start()

    def sum_second(u):
        for half in range(2):
            mine = y if half == 0 else x
            t = send2[u, half, mine].astype(F32)
            for d in range(3):
                second_copy(u, half, d).wait_recv()
                t = t + recv2[u, half, d].astype(F32)
            out[u // 2][u % 2, half * HALF : (half + 1) * HALF, :] = t.astype(BF)

    build_kron(0)
    build_kron(1)
    local[0].wait()
    cross_in(0, 2, 0).wait_recv()
    cross_in(0, 2, 1).wait_recv()
    mix_chip(0, z)
    for n in range(LAST + 1):
        gather_step(0, n)
        if n == 0:
            local[2].wait()
            build_rows(0)
        if n == 2:
            local[3].wait()
            build_rows(1)
        if n == LAST - 1:
            gather_start(1)
        if n % 2 == 1:
            cross_wait(0, n - 1)
            cross_wait(0, n)
            mix_chip(0, lax.rem(z + NZ - n // 2 - 1, NZ))
            mix_chip(0, lax.rem(z + n // 2 + 1, NZ))
    cross_wait(0, LAST)
    mix_chip(0, lax.rem(z + NZ // 2, NZ))

    multiply(0, 0, [functools.partial(gather_step, 1, n) for n in range(4)])
    for half in range(2):
        contract(0, 0, half)
        send_first(0, half)
    multiply(0, 1, [functools.partial(gather_step, 1, n) for n in range(4, 7)])
    for half in range(2):
        contract(0, 1, half)
        send_first(1, half)

    local[1].wait()
    for n in range(2):
        cross_in(1, 2, n).wait_recv()
    for n in range(LAST + 1):
        cross_wait(1, n)
    sum_first(0)

    def mix_right(lo, hi):
        def body(chip, carry):
            mix_chip(1, chip)
            return carry

        lax.fori_loop(lo, hi, body, 0)

    mix_right(0, NZ // 2)
    sum_first(1)
    mix_right(NZ // 2, NZ)
    for k in range(2):
        multiply(1, k)
        for half in range(2):
            contract(1, k, half)
            send_first(2 + k, half)
        sum_second(k)
    for u in (2, 3):
        sum_first(u)
    for u in (2, 3):
        sum_second(u)

    for side in range(2):
        for n in range(LAST + 1):
            for way in range(2):
                ring(side, way, n).wait_send()
                cross(side, way, n).wait_send()
        for n in range(2):
            cross(side, 2, n).wait_send()
    for u in range(4):
        for half in range(2):
            for d in range(3):
                first_copy(u, half, d).wait_send()
                second_copy(u, half, d).wait_send()


def per_device(
    env_left, env_right, site_left, site_right, source_left, source_right, channel_left, channel_right,
    fanin_left, fanin_right, operator_table, operator_pattern,
):
    smem = pl.BlockSpec(memory_space=pltpu.SMEM)
    vmem = pl.BlockSpec(memory_space=pltpu.VMEM)
    hbm = pl.BlockSpec(memory_space=pl.ANY)
    dma = pltpu.SemaphoreType.DMA
    new_left, new_right = pl.pallas_call(
        kernel,
        out_shape=[jax.ShapeDtypeStruct((2, WR, S), BF)] * 2,
        in_specs=[smem] * 6 + [vmem] * 4 + [hbm] * 4,
        out_specs=[vmem, vmem],
        scratch_shapes=[
            pltpu.VMEM((2, 2 * NZ, 2, WR, S), BF),
            pltpu.VMEM((2, 2 * SLOTS, S, S), BF),
            pltpu.VMEM((2, CHANNELS, WR, WR), BF),
            pltpu.VMEM((2 * NZ * CHANNELS, WR, S), BF),
            pltpu.VMEM((W, SLOTS * R, S), BF),
            pltpu.VMEM((2, 2, S, SLOTS * R), BF),
            pltpu.VMEM((4, 2, 4, 4, HALF, S), BF),
            pltpu.VMEM((4, 2, 3, 4, HALF, S), BF),
            pltpu.VMEM((4, 2, 4, HALF, S), BF),
            pltpu.VMEM((4, 2, 3, HALF, S), BF),
            dma((4,)),
            dma((2, 2, LAST + 1)),
            dma((2, 2, LAST + 1)),
            dma((2, 2 * NZ)),
            dma((2, 2 * NZ)),
            dma((4, 2, 3)),
            dma((4, 2, 3)),
            dma((4, 2, 3)),
            dma((4, 2, 3)),
        ],
        compiler_params=pltpu.CompilerParams(
            collective_id=0, has_side_effects=True, vmem_limit_bytes=60 * 2**20
        ),
    )(
        fanin_left, fanin_right, source_left, source_right, channel_left, channel_right,
        source_left.reshape(1, -1), source_right.reshape(1, -1), operator_table, operator_pattern,
        env_left.reshape(2, WR, S), env_right.reshape(2, WR, S), site_left, site_right,
    )
    return new_left.reshape(2, W, R, S), new_right.reshape(2, W, R, S)


def solution(mesh):
    wide, flat = P("sec", None, "env", None), P("sec")
    return jax.shard_map(
        per_device,
        mesh=mesh,
        in_specs=(wide, wide, P("sec", None, None), P("sec", None, None)) + (flat,) * 6 + (P(), P()),
        out_specs=(wide, wide),
        check_vma=False,
    )
```

```python
import functools

import jax
import jax.numpy as jnp
from jax import lax
from jax.experimental import pallas as pl
from jax.experimental.pallas import tpu as pltpu
from jax.sharding import PartitionSpec as P

MESH = pl.DeviceIdType.MESH
BF, F32 = jnp.bfloat16, jnp.float32
NZ, NX, NY = 8, 4, 4
LAST = NZ - 2
W, R, S = 40, 8, 128
WR = W * R
HALF = WR // 2
SLOTS, CHANNELS = 64, 8


def dot(a, b):
    return lax.dot_general(a, b, (((1,), (0,)), ((), ())), preferred_element_type=F32)


def kernel(
    fan_l, fan_r, src_l, src_r, chn_l, chn_r, srcv_l, srcv_r, table, pattern, env_l, env_r, site_l, site_r,
    out_l, out_r,
    got, site, kron, mixenv, mixed, rows_t, send1, recv1, send2, recv2,
    slot_at, source_of, loc_sem, ring_s, ring_r, cross_s, cross_r, s1_s, s1_r, s2_s, s2_r,
):
    fan, src, chn, srcv = (fan_l, fan_r), (src_l, src_r), (chn_l, chn_r), (srcv_l, srcv_r)
    env_in, site_in, out = (env_l, env_r), (site_l, site_r), (out_l, out_r)
    sec, env = lax.axis_index("sec"), lax.axis_index("env")
    z, core = sec // 2, sec % 2
    y, x = env // NX, env % NX
    other = (z * 2 + 1 - core, env)
    up = (lax.rem(z + 1, NZ) * 2 + core, env)
    down = (lax.rem(z + NZ - 1, NZ) * 2 + core, env)
    x_peer = [(sec, y * NX + lax.rem(x + d, NX)) for d in range(1, NX)]
    y_peer = [(sec, lax.rem(y + d, NY) * NX + x) for d in range(1, NY)]

    barrier = pltpu.get_barrier_semaphore()
    partners = [other, up, down] + x_peer + y_peer
    for peer in partners:
        pl.semaphore_signal(barrier, inc=1, device_id=peer, device_id_type=MESH)
    pl.semaphore_wait(barrier, len(partners))

    def remote(a, b, ssem, rsem, peer):
        return pltpu.make_async_remote_copy(
            src_ref=a, dst_ref=b, send_sem=ssem, recv_sem=rsem, device_id=peer, device_id_type=MESH
        )

    def chunk_of(way, n):
        far = n // 2 + 1
        chip = lax.rem(z + NZ - far, NZ) if way == 0 else lax.rem(z + far, NZ)
        h = n % 2 if n < LAST else way
        return chip, h

    def ring(side, way, n):
        peer = up if way == 0 else down
        if n < 2:
            a, chip, h = env_in[side].at[n], z, n
        else:
            back = n - 2 if (n < LAST or way == 0) else n - 1
            chip, h = chunk_of(way, back)
            a = got.at[side, chip * 2 + core, h]
        return remote(a, got.at[side, chip * 2 + core, h], ring_s.at[side, way, n], ring_r.at[side, way, n], peer)

    def ring_in(side, way, n):
        chip, h = chunk_of(way, n)
        spot = got.at[side, chip * 2 + core, h]
        return remote(spot, spot, ring_s.at[side, way, n], ring_r.at[side, way, n], up if way == 0 else down)

    def cross(side, way, n):
        if way == 2:
            a, chip, h, c = env_in[side].at[n], z, n, n
        else:
            chip, h = chunk_of(way, n)
            a, c = got.at[side, chip * 2 + core, h], 2 + 2 * n + way
        return remote(a, got.at[side, chip * 2 + core, h], cross_s.at[side, c], cross_r.at[side, c], other)

    def cross_in(side, way, n):
        chip, h, c = (z, n, n) if way == 2 else (*chunk_of(way, n), 2 + 2 * n + way)
        spot = got.at[side, chip * 2 + 1 - core, h]
        return remote(spot, spot, cross_s.at[side, c], cross_r.at[side, c], other)

    def gather_start(side):
        for n in range(2):
            ring(side, 0, n).start()
            ring(side, 1, n).start()
        for n in range(2):
            cross(side, 2, n).start()

    def gather_step(side, n):
        for way in range(2):
            ring_in(side, way, n).wait_recv()
            for later in range(2, LAST + 1):
                back = later - 2 if (later < LAST or way == 0) else later - 1
                if back == n:
                    ring(side, way, later).start()
            cross(side, way, n).start()

    def cross_wait(side, n):
        for way in range(2):
            cross_in(side, way, n).wait_recv()

    local = [
        pltpu.make_async_copy(env_in[0], got.at[0, sec], loc_sem.at[0]),
        pltpu.make_async_copy(env_in[1], got.at[1, sec], loc_sem.at[1]),
        pltpu.make_async_copy(site_in[0], site.at[0], loc_sem.at[2]),
        pltpu.make_async_copy(site_in[1], site.at[1], loc_sem.at[3]),
    ]
    gather_start(0)
    for c in local:
        c.start()

    spread = (lax.broadcasted_iota(jnp.int32, (WR, W), 0) >> 3 == lax.broadcasted_iota(jnp.int32, (WR, W), 1))
    spread = spread.astype(F32).astype(BF)
    spread_t = (lax.broadcasted_iota(jnp.int32, (W, WR), 1) >> 3 == lax.broadcasted_iota(jnp.int32, (W, WR), 0))
    spread_t = spread_t.astype(F32).astype(BF)
    same_row = (
        lax.broadcasted_iota(jnp.int32, (WR, WR), 0) & 7 == lax.broadcasted_iota(jnp.int32, (WR, WR), 1) & 7
    )

    def build_kron(side, lo, hi):
        def body(p, carry):
            op = (table[p].astype(F32) * pattern[p].astype(F32)).astype(BF)
            dims = (((1,), (1,)), ((), ())) if side == 0 else (((1,), (0,)), ((), ()))
            tall = lax.dot_general(spread, op, dims, preferred_element_type=F32).astype(BF)
            full = jnp.where(same_row, dot(tall, spread_t), 0.0).astype(BF)
            kron[side, p] = full
            return carry

        lax.fori_loop(lo, hi, body, 0, unroll=4)

    def build_rows(side):
        pair_row = pl.multiple_of(env // 2 * 16, 16)
        upper = (env % 2).astype(F32)

        for k in range(2):
            live = fan[side][k]

            def body(g, carry, k=k, live=live):
                block = site[side, pl.ds(k * SLOTS + g * 16, 16), pl.ds(pair_row, 16), :].astype(F32)
                mine = block[:, :R] * (1.0 - upper) + block[:, R:] * upper
                slot = g * 16 + lax.broadcasted_iota(jnp.int32, (16, R, S), 0)
                mine = jnp.where(slot < live, mine, 0.0)
                rows_t[side, k, g] = mine.reshape(16 * R, S).T.astype(BF)
                return carry

            lax.fori_loop(0, SLOTS // 16, body, 0)

    def pick(side, q):
        odd = jnp.max((source_of[side] == 2 * q + 1).astype(F32), axis=1, keepdims=True)
        return (got[side, q, 0].astype(F32) * (1.0 - odd) + got[side, q, 1].astype(F32) * odd).astype(BF)

    def mix_chip(side, chip):
        rhs = jnp.concatenate([pick(side, chip * 2), pick(side, chip * 2 + 1)], axis=1)

        def body(p, carry):
            r = dot(kron[side, p], rhs).astype(BF)
            mixenv[chip * 2 * CHANNELS + p] = r[:, :S]
            mixenv[(chip * 2 + 1) * CHANNELS + p] = r[:, S:]
            return carry

        lax.fori_loop(0, CHANNELS, body, 0, unroll=True)

    def multiply(side, k, hook):
        def part(seg, carry):
            for i in range(8):
                pair = seg * 8 + i
                j = k * SLOTS + 2 * pair
                r0 = dot(mixenv[slot_at[side, j]], site[side, j]).reshape(W, R, S)
                r1 = dot(mixenv[slot_at[side, j + 1]], site[side, j + 1]).reshape(W, R, S)
                both = jnp.concatenate([r0, r1], axis=1).astype(BF)
                mixed[:, pl.ds(pl.multiple_of(pair * 16, 16), 16), :] = both
            hook(seg)
            return carry

        lax.fori_loop(0, SLOTS // 16, part, 0)

    def contract(side, k, half):
        u = side * 2 + k
        left = jnp.concatenate([rows_t[side, k, g] for g in range(SLOTS // 16)], axis=1)
        for i in range(W // 4):
            v = half * (W // 2) + 2 * i
            r = dot(left, jnp.concatenate([mixed[v], mixed[v + 1]], axis=1))
            for e in range(NX * NY):
                t = r[e * R : (e + 1) * R]
                t = jnp.concatenate([t[:, :S], t[:, S:]], axis=0).astype(BF)
                a = (1 - half) * (e % NX) + half * (e // NX)
                b = (1 - half) * (e // NX) + half * (e % NX)
                send1[u, half, a, b, i * 16 : (i + 1) * 16, :] = t

    def along(half, d):
        on_x, on_y = lax.rem(x + d + 1, NX), lax.rem(y + d + 1, NY)
        to_x, to_y = y * NX + on_x, on_y * NX + x
        first = (1 - half) * on_x + half * on_y, (sec, (1 - half) * to_x + half * to_y)
        second = (1 - half) * on_y + half * on_x, (sec, (1 - half) * to_y + half * to_x)
        return first, second

    def first_copy(u, half, c):
        ahead = c in (0, 2, 4)
        spot = along(half, 1)[0][0] if c < 2 else along(half, 0 if ahead else 2)[0][0]
        part = pl.ds(0 if c in (0, 3, 4) else 2, 2)
        return remote(
            send1.at[u, half, spot, part], recv1.at[u, half, c],
            s1_s.at[u, half, c], s1_r.at[u, half, c], along(half, 0 if ahead else 2)[0][1],
        )

    def second_copy(u, half, d):
        spot, peer = along(half, d)[1]
        return remote(send2.at[u, half, spot], recv2.at[u, half, d], s2_s.at[u, half, d], s2_r.at[u, half, d], peer)

    def send_first(u, half):
        for c in range(4):
            first_copy(u, half, c).start()

    def pass_on(u):
        def body(half, carry):
            for c in range(2):
                first_copy(u, half, c).wait_recv()
                spot = along(half, 2 * c)[0][0]
                for b in range(2):
                    t = send1[u, half, spot, 2 * c + b].astype(F32) + recv1[u, half, c, b].astype(F32)
                    send1[u, half, spot, 2 * c + b] = t.astype(BF)
                first_copy(u, half, 4 + c).start()
            return carry

        lax.fori_loop(0, 2, body, 0)

    def sum_first(u):
        def body(half, carry):
            mine = (1 - half) * x + half * y
            for c in range(2, 6):
                first_copy(u, half, c).wait_recv()
            for b in range(4):
                one, two = (3, 4) if b < 2 else (2, 5)
                t = send1[u, half, mine, b].astype(F32)
                t = t + recv1[u, half, one, b % 2].astype(F32) + recv1[u, half, two, b % 2].astype(F32)
                send2[u, half, b] = t.astype(BF)
            for d in range(3):
                second_copy(u, half, d).start()
            return carry

        lax.fori_loop(0, 2, body, 0)

    def sum_second(u):
        for half in range(2):
            mine = y if half == 0 else x
            t = send2[u, half, mine].astype(F32)
            for d in range(3):
                second_copy(u, half, d).wait_recv()
                t = t + recv2[u, half, d].astype(F32)
            out[u // 2][u % 2, half * HALF : (half + 1) * HALF, :] = t.astype(BF)

    for side in range(2):
        source_of[side] = srcv[side][...]

        def place(j, carry, side=side):
            slot_at[side, j] = (src[side][j] >> 1) * CHANNELS + chn[side][j]
            return carry

        lax.fori_loop(0, 2 * SLOTS, place, 0, unroll=8)
    build_kron(0, 0, CHANNELS)
    local[0].wait()

    def before_mix(side, i):
        def at(which, step):
            return pl.when((side == which) & (i == step))

        @at(0, 0)
        def _():
            gather_step(0, 0)

        @at(0, 1)
        def _():
            gather_step(0, 1)

        @at(0, 3)
        def _():
            gather_step(0, 2)
            local[2].wait()
            build_rows(0)
            gather_step(0, 3)

        @at(0, 5)
        def _():
            gather_step(0, 4)
            build_kron(1, 0, CHANNELS)
            gather_step(0, 5)
            gather_start(1)

        @at(0, 7)
        def _():
            gather_step(0, 6)

        @at(1, 0)
        def _():
            local[1].wait()

        @at(1, 1)
        def _():
            gather_step(1, 4)

        @at(1, 2)
        def _():
            pass_on(1)

        @at(1, 3)
        def _():
            gather_step(1, 5)

        @at(1, 4)
        def _():
            sum_first(0)

        @at(1, 5)
        def _():
            gather_step(1, 6)

        @at(1, 7)
        def _():
            sum_first(1)

        @pl.when(i == 0)
        def _():
            cross_in(side, 2, 0).wait_recv()
            cross_in(side, 2, 1).wait_recv()

        for n in range(0, LAST, 2):

            @pl.when(i == n + 1)
            def _(n=n):
                cross_wait(side, n)
                cross_wait(side, n + 1)

        @pl.when(i == LAST + 1)
        def _():
            cross_wait(side, LAST)

    def one_side(side, carry):
        def mix_one(i, carry):
            before_mix(side, i)
            far = (i + 1) // 2
            mix_chip(side, lax.rem(z + NZ + far * (1 - 2 * (i % 2)), NZ))
            return carry

        lax.fori_loop(0, NZ, mix_one, 0)

        def one_sector(k, carry):
            def during(seg):
                @pl.when((side == 0) & (k == 0) & (seg == 3))
                def _():
                    gather_step(1, 0)

                @pl.when((side == 0) & (k == 1) & (seg == 0))
                def _():
                    gather_step(1, 1)

                @pl.when((side == 0) & (k == 1) & (seg == 2))
                def _():
                    gather_step(1, 2)

                @pl.when((side == 1) & (k == 1) & (seg == 3))
                def _():
                    pass_on(2)

            multiply(side, k, during)

            def one_half(half, carry):
                contract(side, k, half)
                send_first(side * 2 + k, half)
                return carry

            lax.fori_loop(0, 2, one_half, 0)

            @pl.when((side == 0) & (k == 1))
            def _():
                pass_on(0)
                gather_step(1, 3)
                local[3].wait()
                build_rows(1)

            @pl.when((side == 1) & (k == 0))
            def _():
                sum_second(0)

            return carry

        lax.fori_loop(0, 2, one_sector, 0)
        return carry

    lax.fori_loop(0, 2, one_side, 0)
    pass_on(3)
    sum_second(1)
    sum_first(2)
    sum_first(3)
    sum_second(2)
    sum_second(3)

    for side in range(2):
        for n in range(LAST + 1):
            for way in range(2):
                ring(side, way, n).wait_send()
                cross(side, way, n).wait_send()
        for n in range(2):
            cross(side, 2, n).wait_send()
    for u in range(4):
        for half in range(2):
            for c in range(6):
                first_copy(u, half, c).wait_send()
            for d in range(3):
                second_copy(u, half, d).wait_send()


def per_device(
    env_left, env_right, site_left, site_right, source_left, source_right, channel_left, channel_right,
    fanin_left, fanin_right, operator_table, operator_pattern,
):
    smem = pl.BlockSpec(memory_space=pltpu.SMEM)
    vmem = pl.BlockSpec(memory_space=pltpu.VMEM)
    hbm = pl.BlockSpec(memory_space=pl.ANY)
    dma = pltpu.SemaphoreType.DMA
    new_left, new_right = pl.pallas_call(
        kernel,
        out_shape=[jax.ShapeDtypeStruct((2, WR, S), BF)] * 2,
        in_specs=[smem] * 6 + [vmem] * 4 + [hbm] * 4,
        out_specs=[vmem, vmem],
        scratch_shapes=[
            pltpu.VMEM((2, 2 * NZ, 2, WR, S), BF),
            pltpu.VMEM((2, 2 * SLOTS, S, S), BF),
            pltpu.VMEM((2, CHANNELS, WR, WR), BF),
            pltpu.VMEM((2 * NZ * CHANNELS, WR, S), BF),
            pltpu.VMEM((W, SLOTS * R, S), BF),
            pltpu.VMEM((2, 2, SLOTS // 16, S, 16 * R), BF),
            pltpu.VMEM((4, 2, 4, 4, HALF, S), BF),
            pltpu.VMEM((4, 2, 6, 2, HALF, S), BF),
            pltpu.VMEM((4, 2, 4, HALF, S), BF),
            pltpu.VMEM((4, 2, 3, HALF, S), BF),
            pltpu.SMEM((2, 2 * SLOTS), jnp.int32),
            pltpu.VMEM((2, 1, 2 * SLOTS), jnp.int32),
            dma((4,)),
            dma((2, 2, LAST + 1)),
            dma((2, 2, LAST + 1)),
            dma((2, 2 * NZ)),
            dma((2, 2 * NZ)),
            dma((4, 2, 6)),
            dma((4, 2, 6)),
            dma((4, 2, 3)),
            dma((4, 2, 3)),
        ],
        compiler_params=pltpu.CompilerParams(
            collective_id=0, has_side_effects=True, vmem_limit_bytes=60 * 2**20
        ),
    )(
        fanin_left, fanin_right, source_left, source_right, channel_left, channel_right,
        source_left.reshape(1, -1), source_right.reshape(1, -1), operator_table, operator_pattern,
        env_left.reshape(2, WR, S), env_right.reshape(2, WR, S), site_left, site_right,
    )
    return new_left.reshape(2, W, R, S), new_right.reshape(2, W, R, S)


def solution(mesh):
    wide, flat = P("sec", None, "env", None), P("sec")
    return jax.shard_map(
        per_device,
        mesh=mesh,
        in_specs=(wide, wide, P("sec", None, None), P("sec", None, None)) + (flat,) * 6 + (P(), P()),
        out_specs=(wide, wide),
        check_vma=False,
    )
```

```python
import functools

import jax
import jax.numpy as jnp
from jax import lax
from jax.experimental import pallas as pl
from jax.experimental.pallas import tpu as pltpu
from jax.sharding import PartitionSpec as P

MESH = pl.DeviceIdType.MESH
BF, F32 = jnp.bfloat16, jnp.float32
NZ, NX, NY = 8, 4, 4
LAST = NZ - 2
W, R, S = 40, 8, 128
WR = W * R
HALF = WR // 2
SLOTS, CHANNELS = 64, 8


def dot(a, b):
    return lax.dot_general(a, b, (((1,), (0,)), ((), ())), preferred_element_type=F32)


def kernel(
    fan_l, fan_r, src_l, src_r, chn_l, chn_r, srcv_l, srcv_r, table, pattern, env_l, env_r, site_l, site_r,
    out_l, out_r,
    got, site, kron, mixenv, mixed, rows_t, send1, recv1, send2, recv2,
    lists, slot_at, source_of, loc_sem, ring_s, ring_r, cross_s, cross_r, s1_s, s1_r, s2_s, s2_r,
):
    fan = (fan_l, fan_r)
    env_in, site_in, out = (env_l, env_r), (site_l, site_r), (out_l, out_r)
    sec, env = lax.axis_index("sec"), lax.axis_index("env")
    z, core = sec // 2, sec % 2
    y, x = env // NX, env % NX
    other = (z * 2 + 1 - core, env)
    up = (lax.rem(z + 1, NZ) * 2 + core, env)
    down = (lax.rem(z + NZ - 1, NZ) * 2 + core, env)
    x_peer = [(sec, y * NX + lax.rem(x + d, NX)) for d in range(1, NX)]
    y_peer = [(sec, lax.rem(y + d, NY) * NX + x) for d in range(1, NY)]

    barrier = pltpu.get_barrier_semaphore()
    partners = [other, up, down] + x_peer + y_peer
    for peer in partners:
        pl.semaphore_signal(barrier, inc=1, device_id=peer, device_id_type=MESH)
    pl.semaphore_wait(barrier, len(partners))

    def remote(a, b, ssem, rsem, peer):
        return pltpu.make_async_remote_copy(
            src_ref=a, dst_ref=b, send_sem=ssem, recv_sem=rsem, device_id=peer, device_id_type=MESH
        )

    def chunk_of(way, n):
        far = n // 2 + 1
        chip = lax.rem(z + NZ - far, NZ) if way == 0 else lax.rem(z + far, NZ)
        h = n % 2 if n < LAST else way
        return chip, h

    def ring(side, way, n, part):
        peer = up if way == 0 else down
        rows = pl.ds(part * HALF, HALF)
        if n < 2:
            a, chip, h = env_in[side].at[n, rows], z, n
        else:
            back = n - 2 if (n < LAST or way == 0) else n - 1
            chip, h = chunk_of(way, back)
            a = got.at[side, chip * 2 + core, h, rows]
        b = got.at[side, chip * 2 + core, h, rows]
        return remote(a, b, ring_s.at[side, way, n, part], ring_r.at[side, way, n, part], peer)

    def ring_in(side, way, n, part):
        chip, h = chunk_of(way, n)
        spot = got.at[side, chip * 2 + core, h, pl.ds(part * HALF, HALF)]
        return remote(spot, spot, ring_s.at[side, way, n, part], ring_r.at[side, way, n, part], up if way == 0 else down)

    def cross(side, way, n):
        if way == 2:
            a, chip, h, c = env_in[side].at[n], z, n, n
        else:
            chip, h = chunk_of(way, n)
            a, c = got.at[side, chip * 2 + core, h], 2 + 2 * n + way
        return remote(a, got.at[side, chip * 2 + core, h], cross_s.at[side, c], cross_r.at[side, c], other)

    def cross_in(side, way, n):
        chip, h, c = (z, n, n) if way == 2 else (*chunk_of(way, n), 2 + 2 * n + way)
        spot = got.at[side, chip * 2 + 1 - core, h]
        return remote(spot, spot, cross_s.at[side, c], cross_r.at[side, c], other)

    def gather_start(side):
        for n in range(2):
            for part in range(2):
                ring(side, 0, n, part).start()
                ring(side, 1, n, part).start()
        for n in range(2):
            cross(side, 2, n).start()

    def gather_step(side, n):
        for part in range(2):
            for way in range(2):
                ring_in(side, way, n, part).wait_recv()
                for later in range(2, LAST + 1):
                    back = later - 2 if (later < LAST or way == 0) else later - 1
                    if back == n:
                        ring(side, way, later, part).start()
        for way in range(2):
            cross(side, way, n).start()

    def cross_wait(side, n):
        for way in range(2):
            cross_in(side, way, n).wait_recv()

    local = [
        pltpu.make_async_copy(env_in[0], got.at[0, sec], loc_sem.at[0]),
        pltpu.make_async_copy(env_in[1], got.at[1, sec], loc_sem.at[1]),
        pltpu.make_async_copy(site_in[0], site.at[0], loc_sem.at[2]),
        pltpu.make_async_copy(site_in[1], site.at[1], loc_sem.at[3]),
    ]
    small = [pltpu.make_async_copy(a, lists.at[i], loc_sem.at[4 + i]) for i, a in enumerate((src_l, src_r, chn_l, chn_r))]
    small += [pltpu.make_async_copy(a, source_of.at[i], loc_sem.at[8 + i]) for i, a in enumerate((srcv_l, srcv_r))]
    gather_start(0)
    for c in small + local:
        c.start()

    spread = (lax.broadcasted_iota(jnp.int32, (WR, W), 0) >> 3 == lax.broadcasted_iota(jnp.int32, (WR, W), 1))
    spread = spread.astype(F32).astype(BF)
    spread_t = (lax.broadcasted_iota(jnp.int32, (W, WR), 1) >> 3 == lax.broadcasted_iota(jnp.int32, (W, WR), 0))
    spread_t = spread_t.astype(F32).astype(BF)
    same_row = (
        lax.broadcasted_iota(jnp.int32, (WR, WR), 0) & 7 == lax.broadcasted_iota(jnp.int32, (WR, WR), 1) & 7
    )

    def build_kron(side, lo, hi):
        def body(p, carry):
            op = (table[p].astype(F32) * pattern[p].astype(F32)).astype(BF)
            dims = (((1,), (1,)), ((), ())) if side == 0 else (((1,), (0,)), ((), ()))
            tall = lax.dot_general(spread, op, dims, preferred_element_type=F32).astype(BF)
            full = jnp.where(same_row, dot(tall, spread_t), 0.0).astype(BF)
            kron[side, p] = full
            return carry

        lax.fori_loop(lo, hi, body, 0, unroll=4)

    def build_rows(side):
        pair_row = pl.multiple_of(env // 2 * 16, 16)
        upper = (env % 2).astype(F32)

        for k in range(2):
            live = fan[side][k]

            def body(g, carry, k=k, live=live):
                block = site[side, pl.ds(k * SLOTS + g * 16, 16), pl.ds(pair_row, 16), :].astype(F32)
                mine = block[:, :R] * (1.0 - upper) + block[:, R:] * upper
                slot = g * 16 + lax.broadcasted_iota(jnp.int32, (16, R, S), 0)
                mine = jnp.where(slot < live, mine, 0.0)
                rows_t[side, k, g] = mine.reshape(16 * R, S).T.astype(BF)
                return carry

            lax.fori_loop(0, SLOTS // 16, body, 0)

    def pick(side, q):
        odd = jnp.max((source_of[side] == 2 * q + 1).astype(F32), axis=1, keepdims=True).astype(BF)
        return got[side, q, 0] * (1 - odd) + got[side, q, 1] * odd

    def mix_chip(side, chip):
        rhs = jnp.concatenate([pick(side, chip * 2), pick(side, chip * 2 + 1)], axis=1)

        def body(p, carry):
            r = dot(kron[side, p], rhs).astype(BF)
            mixenv[chip * 2 * CHANNELS + p] = r[:, :S]
            mixenv[(chip * 2 + 1) * CHANNELS + p] = r[:, S:]
            return carry

        lax.fori_loop(0, CHANNELS, body, 0, unroll=True)

    def multiply(side, k, hook):
        def part(seg, carry):
            for i in range(16):
                pair = seg * 16 + i
                j = k * SLOTS + 2 * pair
                r0 = dot(mixenv[slot_at[side, j]], site[side, j]).reshape(W, R, S)
                r1 = dot(mixenv[slot_at[side, j + 1]], site[side, j + 1]).reshape(W, R, S)
                both = jnp.concatenate([r0, r1], axis=1).astype(BF)
                mixed[:, pl.ds(pl.multiple_of(pair * 16, 16), 16), :] = both
            hook(seg)
            return carry

        lax.fori_loop(0, SLOTS // 32, part, 0)

    def contract(side, k, half):
        u = side * 2 + k
        left = jnp.concatenate([rows_t[side, k, g] for g in range(SLOTS // 16)], axis=1)
        for i in range(W // 4):
            v = half * (W // 2) + 2 * i
            r = dot(left, jnp.concatenate([mixed[v], mixed[v + 1]], axis=1))
            for e in range(NX * NY):
                t = r[e * R : (e + 1) * R]
                t = jnp.concatenate([t[:, :S], t[:, S:]], axis=0).astype(BF)
                a = (1 - half) * (e % NX) + half * (e // NX)
                b = (1 - half) * (e // NX) + half * (e % NX)
                send1[u, half, a, b, i * 16 : (i + 1) * 16, :] = t

    def along(half, d):
        on_x, on_y = lax.rem(x + d + 1, NX), lax.rem(y + d + 1, NY)
        to_x, to_y = y * NX + on_x, on_y * NX + x
        first = (1 - half) * on_x + half * on_y, (sec, (1 - half) * to_x + half * to_y)
        second = (1 - half) * on_y + half * on_x, (sec, (1 - half) * to_y + half * to_x)
        return first, second

    def first_copy(u, half, c):
        ahead = c in (0, 2, 4)
        spot = along(half, 1)[0][0] if c < 2 else along(half, 0 if ahead else 2)[0][0]
        part = pl.ds(0 if c in (0, 3, 4) else 2, 2)
        return remote(
            send1.at[u, half, spot, part], recv1.at[u, half, c],
            s1_s.at[u, half, c], s1_r.at[u, half, c], along(half, 0 if ahead else 2)[0][1],
        )

    def second_copy(u, half, d):
        spot, peer = along(half, d)[1]
        return remote(send2.at[u, half, spot], recv2.at[u, half, d], s2_s.at[u, half, d], s2_r.at[u, half, d], peer)

    def send_first(u, half):
        for c in range(4):
            first_copy(u, half, c).start()

    def pass_on(u):
        def body(half, carry):
            for c in range(2):
                first_copy(u, half, c).wait_recv()
                spot = along(half, 2 * c)[0][0]
                for b in range(2):
                    t = send1[u, half, spot, 2 * c + b].astype(F32) + recv1[u, half, c, b].astype(F32)
                    send1[u, half, spot, 2 * c + b] = t.astype(BF)
                first_copy(u, half, 4 + c).start()
            return carry

        lax.fori_loop(0, 2, body, 0)

    def sum_first(u):
        def body(half, carry):
            mine = (1 - half) * x + half * y
            for c in range(2, 6):
                first_copy(u, half, c).wait_recv()
            for b in range(4):
                one, two = (3, 4) if b < 2 else (2, 5)
                t = send1[u, half, mine, b].astype(F32)
                t = t + recv1[u, half, one, b % 2].astype(F32) + recv1[u, half, two, b % 2].astype(F32)
                send2[u, half, b] = t.astype(BF)
            for d in range(3):
                second_copy(u, half, d).start()
            return carry

        lax.fori_loop(0, 2, body, 0)

    def sum_second(u):
        for half in range(2):
            mine = y if half == 0 else x
            t = send2[u, half, mine].astype(F32)
            for d in range(3):
                second_copy(u, half, d).wait_recv()
                t = t + recv2[u, half, d].astype(F32)
            out[u // 2][u % 2, half * HALF : (half + 1) * HALF, :] = t.astype(BF)

    build_kron(0, 0, CHANNELS)
    for c in small:
        c.wait()
    for side in range(2):

        def place(j, carry, side=side):
            slot_at[side, j] = (lists[side, j] >> 1) * CHANNELS + lists[2 + side, j]
            return carry

        lax.fori_loop(0, 2 * SLOTS, place, 0, unroll=8)
    local[0].wait()

    def before_mix(side, i):
        def at(which, step):
            return pl.when((side == which) & (i == step))

        @at(0, 0)
        def _():
            gather_step(0, 0)

        @at(0, 1)
        def _():
            gather_step(0, 1)

        @at(0, 3)
        def _():
            gather_step(0, 2)
            local[2].wait()
            build_rows(0)
            gather_step(0, 3)

        @at(0, 5)
        def _():
            gather_step(0, 4)
            build_kron(1, 0, CHANNELS)
            gather_step(0, 5)
            gather_start(1)

        @at(0, 7)
        def _():
            gather_step(0, 6)

        @at(1, 0)
        def _():
            local[1].wait()

        @at(1, 1)
        def _():
            gather_step(1, 3)

        @at(1, 2)
        def _():
            pass_on(0)
            gather_step(1, 4)

        @at(1, 4)
        def _():
            pass_on(1)
            gather_step(1, 5)

        @at(1, 6)
        def _():
            gather_step(1, 6)

        @pl.when(i == 0)
        def _():
            cross_in(side, 2, 0).wait_recv()
            cross_in(side, 2, 1).wait_recv()

        for n in range(0, LAST, 2):

            @pl.when(i == n + 1)
            def _(n=n):
                cross_wait(side, n)
                cross_wait(side, n + 1)

        @pl.when(i == LAST + 1)
        def _():
            cross_wait(side, LAST)

    def one_side(side, carry):
        def mix_one(i, carry):
            before_mix(side, i)
            far = (i + 1) // 2
            mix_chip(side, lax.rem(z + NZ + far * (1 - 2 * (i % 2)), NZ))
            return carry

        lax.fori_loop(0, NZ, mix_one, 0)

        def one_sector(k, carry):
            def during(seg):
                @pl.when((side == 0) & (k == 0) & (seg == 1))
                def _():
                    gather_step(1, 0)

                @pl.when((side == 0) & (k == 1) & (seg == 0))
                def _():
                    gather_step(1, 1)

                @pl.when((side == 1) & (k == 0) & (seg == 0))
                def _():
                    sum_first(0)

            multiply(side, k, during)

            def one_half(half, carry):
                contract(side, k, half)
                send_first(side * 2 + k, half)

                @pl.when((side == 0) & (k == 1) & (half == 0))
                def _():
                    gather_step(1, 2)

                @pl.when((side == 1) & (k == 1) & (half == 0))
                def _():
                    pass_on(2)

                return carry

            lax.fori_loop(0, 2, one_half, 0)

            @pl.when((side == 0) & (k == 1))
            def _():
                local[3].wait()
                build_rows(1)

            @pl.when((side == 1) & (k == 0))
            def _():
                sum_first(1)

            return carry

        lax.fori_loop(0, 2, one_sector, 0)
        return carry

    lax.fori_loop(0, 2, one_side, 0)
    sum_second(0)
    sum_second(1)
    pass_on(3)
    sum_first(2)
    sum_first(3)
    sum_second(2)
    sum_second(3)

    for side in range(2):
        for n in range(LAST + 1):
            for way in range(2):
                ring(side, way, n, 0).wait_send()
                ring(side, way, n, 1).wait_send()
                cross(side, way, n).wait_send()
        for n in range(2):
            cross(side, 2, n).wait_send()
    for u in range(4):
        for half in range(2):
            for c in range(6):
                first_copy(u, half, c).wait_send()
            for d in range(3):
                second_copy(u, half, d).wait_send()


def hand_out(a, b, out_a, out_b):
    out_a[...] = a[...]
    out_b[...] = b[...]


def per_device(
    env_left, env_right, site_left, site_right, source_left, source_right, channel_left, channel_right,
    fanin_left, fanin_right, operator_table, operator_pattern,
):
    smem = pl.BlockSpec(memory_space=pltpu.SMEM)
    vmem = pl.BlockSpec(memory_space=pltpu.VMEM)
    hbm = pl.BlockSpec(memory_space=pl.ANY)
    dma = pltpu.SemaphoreType.DMA
    new_left, new_right = pl.pallas_call(
        kernel,
        out_shape=[jax.ShapeDtypeStruct((2, WR, S), BF)] * 2,
        in_specs=[smem] * 2 + [hbm] * 6 + [vmem] * 2 + [hbm] * 4,
        out_specs=[vmem, vmem],
        scratch_shapes=[
            pltpu.VMEM((2, 2 * NZ, 2, WR, S), BF),
            pltpu.VMEM((2, 2 * SLOTS, S, S), BF),
            pltpu.VMEM((2, CHANNELS, WR, WR), BF),
            pltpu.VMEM((2 * NZ * CHANNELS, WR, S), BF),
            pltpu.VMEM((W, SLOTS * R, S), BF),
            pltpu.VMEM((2, 2, SLOTS // 16, S, 16 * R), BF),
            pltpu.VMEM((4, 2, 4, 4, HALF, S), BF),
            pltpu.VMEM((4, 2, 6, 2, HALF, S), BF),
            pltpu.VMEM((4, 2, 4, HALF, S), BF),
            pltpu.VMEM((4, 2, 3, HALF, S), BF),
            pltpu.SMEM((4, 2 * SLOTS), jnp.int32),
            pltpu.SMEM((2, 2 * SLOTS), jnp.int32),
            pltpu.VMEM((2, 1, 2 * SLOTS), jnp.int32),
            dma((10,)),
            dma((2, 2, LAST + 1, 2)),
            dma((2, 2, LAST + 1, 2)),
            dma((2, 2 * NZ)),
            dma((2, 2 * NZ)),
            dma((4, 2, 6)),
            dma((4, 2, 6)),
            dma((4, 2, 3)),
            dma((4, 2, 3)),
        ],
        compiler_params=pltpu.CompilerParams(
            collective_id=0, has_side_effects=True, vmem_limit_bytes=60 * 2**20
        ),
    )(
        fanin_left, fanin_right, source_left, source_right, channel_left, channel_right,
        source_left.reshape(1, -1), source_right.reshape(1, -1), operator_table, operator_pattern,
        env_left.reshape(2, WR, S), env_right.reshape(2, WR, S), site_left, site_right,
    )
    new_left, new_right = pl.pallas_call(
        hand_out,
        out_shape=[jax.ShapeDtypeStruct((2, WR, S), BF)] * 2,
        in_specs=[vmem, vmem],
        out_specs=[vmem, vmem],
    )(new_left, new_right)
    return new_left.reshape(2, W, R, S), new_right.reshape(2, W, R, S)


def solution(mesh):
    wide, flat = P("sec", None, "env", None), P("sec")
    return jax.shard_map(
        per_device,
        mesh=mesh,
        in_specs=(wide, wide, P("sec", None, None), P("sec", None, None)) + (flat,) * 6 + (P(), P()),
        out_specs=(wide, wide),
        check_vma=False,
    )
```

```python
import functools

import jax
import jax.numpy as jnp
from jax import lax
from jax.experimental import pallas as pl
from jax.experimental.pallas import tpu as pltpu
from jax.sharding import PartitionSpec as P

MESH = pl.DeviceIdType.MESH
BF, F32 = jnp.bfloat16, jnp.float32
NZ, NX, NY = 8, 4, 4
LAST = NZ - 2
W, R, S = 40, 8, 128
WR = W * R
HALF = WR // 2
SLOTS, CHANNELS = 64, 8


def dot(a, b):
    return lax.dot_general(a, b, (((1,), (0,)), ((), ())), preferred_element_type=F32)


def kernel(
    fan_l, fan_r, src_l, src_r, chn_l, chn_r, srcv_l, srcv_r, table, pattern, env_l, env_r, site_l, site_r,
    out_l, out_r,
    got, site, kron, mixenv, mixed, rows_t, send1, recv1, send2, recv2,
    lists, slot_at, source_of, loc_sem, ring_s, ring_r, cross_s, cross_r, s1_s, s1_r, s2_s, s2_r,
):
    fan = (fan_l, fan_r)
    env_in, site_in, out = (env_l, env_r), (site_l, site_r), (out_l, out_r)
    sec, env = lax.axis_index("sec"), lax.axis_index("env")
    z, core = sec // 2, sec % 2
    y, x = env // NX, env % NX
    other = (z * 2 + 1 - core, env)
    up = (lax.rem(z + 1, NZ) * 2 + core, env)
    down = (lax.rem(z + NZ - 1, NZ) * 2 + core, env)
    x_peer = [(sec, y * NX + lax.rem(x + d, NX)) for d in range(1, NX)]
    y_peer = [(sec, lax.rem(y + d, NY) * NX + x) for d in range(1, NY)]

    barrier = pltpu.get_barrier_semaphore()
    partners = [other, up, down] + x_peer + y_peer
    for peer in partners:
        pl.semaphore_signal(barrier, inc=1, device_id=peer, device_id_type=MESH)
    local = [
        pltpu.make_async_copy(env_in[0], got.at[0, sec], loc_sem.at[0]),
        pltpu.make_async_copy(env_in[1], got.at[1, sec], loc_sem.at[1]),
        pltpu.make_async_copy(site_in[0], site.at[0], loc_sem.at[2]),
        pltpu.make_async_copy(site_in[1], site.at[1], loc_sem.at[3]),
    ]
    small = [pltpu.make_async_copy(a, lists.at[i], loc_sem.at[4 + i]) for i, a in enumerate((src_l, src_r, chn_l, chn_r))]
    small += [pltpu.make_async_copy(a, source_of.at[i], loc_sem.at[8 + i]) for i, a in enumerate((srcv_l, srcv_r))]
    for c in small + local:
        c.start()
    pl.semaphore_wait(barrier, len(partners))

    def remote(a, b, ssem, rsem, peer):
        return pltpu.make_async_remote_copy(
            src_ref=a, dst_ref=b, send_sem=ssem, recv_sem=rsem, device_id=peer, device_id_type=MESH
        )

    def chunk_of(way, n):
        far = n // 2 + 1
        chip = lax.rem(z + NZ - far, NZ) if way == 0 else lax.rem(z + far, NZ)
        h = n % 2 if n < LAST else way
        return chip, h

    def ring(side, way, n, part):
        peer = up if way == 0 else down
        rows = pl.ds(part * HALF, HALF)
        if n < 2:
            a, chip, h = env_in[side].at[n, rows], z, n
        else:
            back = n - 2 if (n < LAST or way == 0) else n - 1
            chip, h = chunk_of(way, back)
            a = got.at[side, chip * 2 + core, h, rows]
        b = got.at[side, chip * 2 + core, h, rows]
        return remote(a, b, ring_s.at[side, way, n, part], ring_r.at[side, way, n, part], peer)

    def ring_in(side, way, n, part):
        chip, h = chunk_of(way, n)
        spot = got.at[side, chip * 2 + core, h, pl.ds(part * HALF, HALF)]
        return remote(spot, spot, ring_s.at[side, way, n, part], ring_r.at[side, way, n, part], up if way == 0 else down)

    def cross(side, way, n):
        if way == 2:
            a, chip, h, c = env_in[side].at[n], z, n, n
        else:
            chip, h = chunk_of(way, n)
            a, c = got.at[side, chip * 2 + core, h], 2 + 2 * n + way
        return remote(a, got.at[side, chip * 2 + core, h], cross_s.at[side, c], cross_r.at[side, c], other)

    def cross_in(side, way, n):
        chip, h, c = (z, n, n) if way == 2 else (*chunk_of(way, n), 2 + 2 * n + way)
        spot = got.at[side, chip * 2 + 1 - core, h]
        return remote(spot, spot, cross_s.at[side, c], cross_r.at[side, c], other)

    def gather_start(side):
        for n in range(2):
            for part in range(2):
                ring(side, 0, n, part).start()
                ring(side, 1, n, part).start()
        for n in range(2):
            cross(side, 2, n).start()

    def gather_step(side, n):
        for part in range(2):
            for way in range(2):
                ring_in(side, way, n, part).wait_recv()
                for later in range(2, LAST + 1):
                    back = later - 2 if (later < LAST or way == 0) else later - 1
                    if back == n:
                        ring(side, way, later, part).start()
        for way in range(2):
            cross(side, way, n).start()

    def cross_wait(side, n):
        for way in range(2):
            cross_in(side, way, n).wait_recv()

    gather_start(0)

    spread = (lax.broadcasted_iota(jnp.int32, (WR, W), 0) >> 3 == lax.broadcasted_iota(jnp.int32, (WR, W), 1))
    spread = spread.astype(F32).astype(BF)
    spread_t = (lax.broadcasted_iota(jnp.int32, (W, WR), 1) >> 3 == lax.broadcasted_iota(jnp.int32, (W, WR), 0))
    spread_t = spread_t.astype(F32).astype(BF)
    same_row = (
        lax.broadcasted_iota(jnp.int32, (WR, WR), 0) & 7 == lax.broadcasted_iota(jnp.int32, (WR, WR), 1) & 7
    )

    def build_kron(side, lo, hi):
        def body(p, carry):
            op = (table[p].astype(F32) * pattern[p].astype(F32)).astype(BF)
            dims = (((1,), (1,)), ((), ())) if side == 0 else (((1,), (0,)), ((), ()))
            tall = lax.dot_general(spread, op, dims, preferred_element_type=F32).astype(BF)
            full = jnp.where(same_row, dot(tall, spread_t), 0.0).astype(BF)
            kron[side, p] = full
            return carry

        lax.fori_loop(lo, hi, body, 0, unroll=4)

    def build_rows(side):
        pair_row = pl.multiple_of(env // 2 * 16, 16)
        upper = (env % 2).astype(F32)

        for k in range(2):
            live = fan[side][k]

            def body(g, carry, k=k, live=live):
                block = site[side, pl.ds(k * SLOTS + g * 16, 16), pl.ds(pair_row, 16), :].astype(F32)
                mine = block[:, :R] * (1.0 - upper) + block[:, R:] * upper
                slot = g * 16 + lax.broadcasted_iota(jnp.int32, (16, R, S), 0)
                mine = jnp.where(slot < live, mine, 0.0)
                rows_t[side, k, g] = mine.reshape(16 * R, S).T.astype(BF)
                return carry

            lax.fori_loop(0, SLOTS // 16, body, 0)

    def pick(side, q):
        odd = jnp.max((source_of[side] == 2 * q + 1).astype(F32), axis=1, keepdims=True).astype(BF)
        return got[side, q, 0] * (1 - odd) + got[side, q, 1] * odd

    def mix_chip(side, chip):
        rhs = jnp.concatenate([pick(side, chip * 2), pick(side, chip * 2 + 1)], axis=1)

        def body(p, carry):
            r = dot(kron[side, p], rhs).astype(BF)
            mixenv[chip * 2 * CHANNELS + p] = r[:, :S]
            mixenv[(chip * 2 + 1) * CHANNELS + p] = r[:, S:]
            return carry

        lax.fori_loop(0, CHANNELS, body, 0, unroll=True)

    def multiply(side, k, hook):
        def part(seg, carry):
            for i in range(16):
                pair = seg * 16 + i
                j = k * SLOTS + 2 * pair
                r0 = dot(mixenv[slot_at[side, j]], site[side, j]).reshape(W, R, S)
                r1 = dot(mixenv[slot_at[side, j + 1]], site[side, j + 1]).reshape(W, R, S)
                both = jnp.concatenate([r0, r1], axis=1).astype(BF)
                mixed[:, pl.ds(pl.multiple_of(pair * 16, 16), 16), :] = both
            hook(seg)
            return carry

        lax.fori_loop(0, SLOTS // 32, part, 0)

    def contract(side, k, half):
        u = side * 2 + k
        left = jnp.concatenate([rows_t[side, k, g] for g in range(SLOTS // 16)], axis=1)
        for i in range(W // 4):
            v = half * (W // 2) + 2 * i
            r = dot(left, jnp.concatenate([mixed[v], mixed[v + 1]], axis=1))
            for e in range(NX * NY):
                t = r[e * R : (e + 1) * R]
                t = jnp.concatenate([t[:, :S], t[:, S:]], axis=0).astype(BF)
                a = (1 - half) * (e % NX) + half * (e // NX)
                b = (1 - half) * (e // NX) + half * (e % NX)
                send1[u, half, a, b, i * 16 : (i + 1) * 16, :] = t

    def along(half, d):
        on_x, on_y = lax.rem(x + d + 1, NX), lax.rem(y + d + 1, NY)
        to_x, to_y = y * NX + on_x, on_y * NX + x
        first = (1 - half) * on_x + half * on_y, (sec, (1 - half) * to_x + half * to_y)
        second = (1 - half) * on_y + half * on_x, (sec, (1 - half) * to_y + half * to_x)
        return first, second

    def first_copy(u, half, c):
        ahead = c in (0, 2, 4)
        spot = along(half, 1)[0][0] if c < 2 else along(half, 0 if ahead else 2)[0][0]
        part = pl.ds(0 if c in (0, 3, 4) else 2, 2)
        return remote(
            send1.at[u, half, spot, part], recv1.at[u, half, c],
            s1_s.at[u, half, c], s1_r.at[u, half, c], along(half, 0 if ahead else 2)[0][1],
        )

    def second_copy(u, half, d):
        spot, peer = along(half, d)[1]
        return remote(send2.at[u, half, spot], recv2.at[u, half, d], s2_s.at[u, half, d], s2_r.at[u, half, d], peer)

    def send_first(u, half):
        for c in range(4):
            first_copy(u, half, c).start()

    def pass_on(u):
        def body(half, carry):
            for c in range(2):
                first_copy(u, half, c).wait_recv()
                spot = along(half, 2 * c)[0][0]
                for b in range(2):
                    t = send1[u, half, spot, 2 * c + b].astype(F32) + recv1[u, half, c, b].astype(F32)
                    send1[u, half, spot, 2 * c + b] = t.astype(BF)
                first_copy(u, half, 4 + c).start()
            return carry

        lax.fori_loop(0, 2, body, 0)

    def sum_first(u):
        def body(half, carry):
            mine = (1 - half) * x + half * y
            for c in range(2, 6):
                first_copy(u, half, c).wait_recv()
            for b in range(4):
                one, two = (3, 4) if b < 2 else (2, 5)
                t = send1[u, half, mine, b].astype(F32)
                t = t + recv1[u, half, one, b % 2].astype(F32) + recv1[u, half, two, b % 2].astype(F32)
                send2[u, half, b] = t.astype(BF)
            for d in range(3):
                second_copy(u, half, d).start()
            return carry

        lax.fori_loop(0, 2, body, 0)

    def sum_second(u):
        for half in range(2):
            mine = y if half == 0 else x
            t = send2[u, half, mine].astype(F32)
            for d in range(3):
                second_copy(u, half, d).wait_recv()
                t = t + recv2[u, half, d].astype(F32)
            out[u // 2][u % 2, half * HALF : (half + 1) * HALF, :] = t.astype(BF)

    build_kron(0, 0, CHANNELS)
    for c in small:
        c.wait()
    for side in range(2):

        def place(j, carry, side=side):
            slot_at[side, j] = (lists[side, j] >> 1) * CHANNELS + lists[2 + side, j]
            return carry

        lax.fori_loop(0, 2 * SLOTS, place, 0, unroll=8)
    local[0].wait()

    def before_mix(side, i):
        def at(which, step):
            return pl.when((side == which) & (i == step))

        @at(0, 0)
        def _():
            gather_step(0, 0)

        @at(0, 1)
        def _():
            gather_step(0, 1)

        @at(0, 3)
        def _():
            gather_step(0, 2)
            local[2].wait()
            build_rows(0)
            gather_step(0, 3)

        @at(0, 5)
        def _():
            gather_step(0, 4)
            gather_step(0, 5)

        @at(0, 7)
        def _():
            gather_step(0, 6)
            gather_start(1)
            build_kron(1, 0, CHANNELS)

        @at(1, 0)
        def _():
            local[1].wait()

        @at(1, 1)
        def _():
            gather_step(1, 3)

        @at(1, 2)
        def _():
            pass_on(0)
            gather_step(1, 4)

        @at(1, 4)
        def _():
            pass_on(1)
            gather_step(1, 5)

        @at(1, 6)
        def _():
            sum_first(0)

        @at(1, 7)
        def _():
            gather_step(1, 6)

        @pl.when(i == 0)
        def _():
            cross_in(side, 2, 0).wait_recv()
            cross_in(side, 2, 1).wait_recv()

        for n in range(0, LAST, 2):

            @pl.when(i == n + 1)
            def _(n=n):
                cross_wait(side, n)
                cross_wait(side, n + 1)

        @pl.when(i == LAST + 1)
        def _():
            cross_wait(side, LAST)

    def one_side(side, carry):
        def mix_one(i, carry):
            before_mix(side, i)
            far = (i + 1) // 2
            mix_chip(side, lax.rem(z + NZ + far * (1 - 2 * (i % 2)), NZ))
            return carry

        lax.fori_loop(0, NZ, mix_one, 0)

        def one_sector(k, carry):
            def during(seg):
                @pl.when((side == 0) & (k == 0) & (seg == 1))
                def _():
                    gather_step(1, 0)

                @pl.when((side == 0) & (k == 1) & (seg == 0))
                def _():
                    gather_step(1, 1)

            multiply(side, k, during)

            def one_half(half, carry):
                contract(side, k, half)
                send_first(side * 2 + k, half)

                @pl.when((side == 0) & (k == 1) & (half == 0))
                def _():
                    gather_step(1, 2)

                @pl.when((side == 1) & (k == 1) & (half == 0))
                def _():
                    pass_on(2)

                return carry

            lax.fori_loop(0, 2, one_half, 0)

            @pl.when((side == 0) & (k == 1))
            def _():
                local[3].wait()
                build_rows(1)

            @pl.when((side == 1) & (k == 0))
            def _():
                sum_first(1)

            return carry

        lax.fori_loop(0, 2, one_sector, 0)
        return carry

    lax.fori_loop(0, 2, one_side, 0)
    def sent(units):
        def body(i, carry):
            u, half = units + i // 2, i % 2
            for c in range(6):
                first_copy(u, half, c).wait_send()
            for d in range(3):
                second_copy(u, half, d).wait_send()
            return carry

        lax.fori_loop(0, 4, body, 0)

    sum_second(0)
    sum_second(1)
    for side in range(2):
        for n in range(LAST + 1):
            for way in range(2):
                ring(side, way, n, 0).wait_send()
                ring(side, way, n, 1).wait_send()
                cross(side, way, n).wait_send()
        for n in range(2):
            cross(side, 2, n).wait_send()
    sent(0)
    pass_on(3)
    sum_first(2)
    sum_first(3)
    sum_second(2)
    sum_second(3)
    sent(2)


def hand_out(a, b, out_a, out_b):
    out_a[...] = a[...]
    out_b[...] = b[...]


def per_device(
    env_left, env_right, site_left, site_right, source_left, source_right, channel_left, channel_right,
    fanin_left, fanin_right, operator_table, operator_pattern,
):
    smem = pl.BlockSpec(memory_space=pltpu.SMEM)
    vmem = pl.BlockSpec(memory_space=pltpu.VMEM)
    hbm = pl.BlockSpec(memory_space=pl.ANY)
    dma = pltpu.SemaphoreType.DMA
    new_left, new_right = pl.pallas_call(
        kernel,
        out_shape=[jax.ShapeDtypeStruct((2, WR, S), BF)] * 2,
        in_specs=[smem] * 2 + [hbm] * 6 + [vmem] * 2 + [hbm] * 4,
        out_specs=[vmem, vmem],
        scratch_shapes=[
            pltpu.VMEM((2, 2 * NZ, 2, WR, S), BF),
            pltpu.VMEM((2, 2 * SLOTS, S, S), BF),
            pltpu.VMEM((2, CHANNELS, WR, WR), BF),
            pltpu.VMEM((2 * NZ * CHANNELS, WR, S), BF),
            pltpu.VMEM((W, SLOTS * R, S), BF),
            pltpu.VMEM((2, 2, SLOTS // 16, S, 16 * R), BF),
            pltpu.VMEM((4, 2, 4, 4, HALF, S), BF),
            pltpu.VMEM((4, 2, 6, 2, HALF, S), BF),
            pltpu.VMEM((4, 2, 4, HALF, S), BF),
            pltpu.VMEM((4, 2, 3, HALF, S), BF),
            pltpu.SMEM((4, 2 * SLOTS), jnp.int32),
            pltpu.SMEM((2, 2 * SLOTS), jnp.int32),
            pltpu.VMEM((2, 1, 2 * SLOTS), jnp.int32),
            dma((10,)),
            dma((2, 2, LAST + 1, 2)),
            dma((2, 2, LAST + 1, 2)),
            dma((2, 2 * NZ)),
            dma((2, 2 * NZ)),
            dma((4, 2, 6)),
            dma((4, 2, 6)),
            dma((4, 2, 3)),
            dma((4, 2, 3)),
        ],
        compiler_params=pltpu.CompilerParams(
            collective_id=0, has_side_effects=True, vmem_limit_bytes=60 * 2**20
        ),
    )(
        fanin_left, fanin_right, source_left, source_right, channel_left, channel_right,
        source_left.reshape(1, -1), source_right.reshape(1, -1), operator_table, operator_pattern,
        env_left.reshape(2, WR, S), env_right.reshape(2, WR, S), site_left, site_right,
    )
    new_left, new_right = pl.pallas_call(
        hand_out,
        out_shape=[jax.ShapeDtypeStruct((2, WR, S), BF)] * 2,
        in_specs=[vmem, vmem],
        out_specs=[vmem, vmem],
    )(new_left, new_right)
    return new_left.reshape(2, W, R, S), new_right.reshape(2, W, R, S)


def solution(mesh):
    wide, flat = P("sec", None, "env", None), P("sec")
    return jax.shard_map(
        per_device,
        mesh=mesh,
        in_specs=(wide, wide, P("sec", None, None), P("sec", None, None)) + (flat,) * 6 + (P(), P()),
        out_specs=(wide, wide),
        check_vma=False,
    )
```
